32 devices in a mesh: day: 8 (over z, core), row: 2 (over y), col: 2 (over x).
Axes of the slice: x: 2, y: 2, z: 4, core: 2. Of those that a mesh axis runs over, the one named last changes fastest.
Arguments:
- traces: bfloat16 [896, 128, 256], P('day', ('col', 'row')), may hold values from -64 to 64
- valid: int32 [896, 128], P('day', ('col', 'row')), may hold values 0 or 1
Outputs:
- cross: float32 [2, 32, 2, 64, 128], P(None, 'day', None, 'row', 'col')
The draws below stay inside these ranges and needn't reach their ends.
All inputs are finite; a program needn't handle non-finite values. No bound on the sum of `valid` on one device may be relied on, other than what follows from the above.
Results may differ from the reference program's by a relative error of at most 0.0025.
Values may be sent and summed in bfloat16 or wider, within the bound.
No kernel may reach another device: no remote copies, remote signals or barrier semaphores. Data moves between devices by JAX's collectives and lax.ppermute only.
A program may use at most 64 MiB of HBM per device.

```python
import math
import jax
import jax.numpy as jnp
from jax import lax

WIN = 112
L = 256
F = 32
K0 = 16
WINDOWS = 896
C = 128
N_DAY = 8
N_COL = 2


def draw_traces(key, part):
    key = jax.random.fold_in(key, 5)
    first, second, third = jax.random.split(key, 3)
    noise = jnp.clip(jax.random.normal(first, (WINDOWS, C, L), jnp.float32), -5.0, 5.0)
    shared = jnp.clip(jax.random.normal(second, (WINDOWS, 1, L), jnp.float32), -5.0, 5.0)
    level = jnp.exp(jax.random.uniform(third, (WINDOWS, C, 1), jnp.float32, 0.0, math.log(10.0)))
    mixing = 0.15
    return (level * (noise + mixing * shared)).astype(jnp.bfloat16)


def with_ends(entries, rng, low, largest):
    spot = [jax.random.randint(jax.random.fold_in(rng, axis), (), 0, length) for axis, length in enumerate(entries.shape)]
    main_axis = entries.shape.index(max(entries.shape))
    next_to = spot[:main_axis] + [(spot[main_axis] + 1) % entries.shape[main_axis]] + spot[main_axis + 1:]
    return entries.at[tuple(spot)].set(low).at[tuple(next_to)].set(largest)


def setup_inputs(seed: int = 0) -> dict:
    streams_of = jax.random.split(jax.random.key(seed), 3)
    traces = draw_traces(jax.random.fold_in(streams_of[2], 71), 0)
    valid = with_ends((jax.random.randint(streams_of[1], (WINDOWS, C), 0, 8) < 7).astype(jnp.int32), jax.random.fold_in(streams_of[1], 1), 0, 1)
    return dict(traces=traces, valid=valid)


def dft_table():
    sample = jnp.arange(L, dtype=jnp.int32)
    bins = K0 + jnp.arange(F, dtype=jnp.int32)
    angle = (sample[:, None] * bins[None, :] % L).astype(jnp.float32) * (2.0 * math.pi / L)
    taper = 0.5 - 0.5 * jnp.cos((sample.astype(jnp.float32) + 0.5) * (2.0 * math.pi / L))
    table = jnp.concatenate([taper[:, None] * jnp.cos(angle), -taper[:, None] * jnp.sin(angle)], axis=1)
    return table.astype(jnp.bfloat16)

def whitened(samples, usable):
    count, width = usable.shape
    spectrum = jnp.dot(samples.reshape(count * width, L), dft_table(), preferred_element_type=jnp.float32)
    energy = lax.optimization_barrier(jnp.mean(spectrum * spectrum, axis=1, keepdims=True))
    scaled = spectrum * lax.rsqrt(energy + 1e-06) * usable.reshape(count * width, 1).astype(jnp.float32)
    white = scaled.astype(jnp.bfloat16).reshape(count, width, 2, F)
    return jnp.transpose(white, (3, 2, 0, 1))

def reference(traces, valid):
    day_traces = traces.reshape(N_DAY, WIN, C, L)
    day_flags = valid.reshape(N_DAY, WIN, C)

    def add_day(total, day_data):
        white = whitened(day_data[0], day_data[1])
        left = white.reshape(F, 2 * WIN, C).astype(jnp.float32)
        turned = jnp.concatenate([white[:, 1], -white[:, 0]], axis=1).astype(jnp.float32)
        real_part = jnp.einsum('fwi,fwj->fij', left, left)
        imag_part = jnp.einsum('fwi,fwj->fij', turned, left)
        return (total + jnp.stack([real_part, imag_part]), None)
    total, _ = lax.scan(add_day, jnp.zeros((2, F, C, C), jnp.float32), (day_traces, day_flags))
    return (total * (1.0 / math.sqrt(WINDOWS))).reshape(2, F, N_COL, C // N_COL, C)
```

```python
import functools
import math

import jax
import jax.numpy as jnp
import numpy as np
from jax import lax
from jax.experimental import pallas as pl
from jax.experimental.pallas import tpu as pltpu
from jax.sharding import PartitionSpec as P

L = 256
F = 32
K0 = 16
LANES = 128


def dft_rows(length, bins):
    sample = np.arange(length, dtype=np.int32)
    bins = np.asarray(bins, dtype=np.int32)
    angle = (sample[None, :] * bins[:, None] % length).astype(np.float32) * np.float32(
        2.0 * math.pi / length
    )
    taper = np.float32(0.5) - np.float32(0.5) * np.cos(
        (sample.astype(np.float32) + np.float32(0.5)) * np.float32(2.0 * math.pi / length)
    )
    table = np.concatenate([taper * np.cos(angle), -taper * np.sin(angle)], axis=0)
    return table.astype(jnp.bfloat16)


def whiten_kernel(
    traces_hbm, valid_hbm, table_hbm, white_ref, traces, valid, table, flags, pieces, sems
):
    chunks, span, channels, length = traces.shape
    nbins = table.shape[0] // 2
    windows = chunks * span
    groups = chunks // 4
    shard = 2 * lax.axis_index("col") + lax.axis_index("row")
    late = lax.axis_index("day") // (lax.axis_size("day") // 2)

    small = [
        pltpu.make_async_copy(valid_hbm, valid, sems.at[groups]),
        pltpu.make_async_copy(table_hbm.at[late], table, sems.at[groups + 1]),
    ]
    large = [
        pltpu.make_async_copy(
            traces_hbm.at[pl.ds(4 * g, 4)], traces.at[pl.ds(4 * g, 4)], sems.at[g]
        )
        for g in range(groups)
    ]
    for copy in small + large:
        copy.start()
    for copy in small:
        copy.wait()

    spread = jnp.concatenate([valid[...].astype(jnp.float32)] * span, axis=0)
    place = lax.broadcasted_iota(jnp.int32, spread.shape, 0) // channels
    window = lax.broadcasted_iota(jnp.int32, spread.shape, 1)
    spread = jnp.where((window + shard) % span == place, spread, 0.0).astype(jnp.bfloat16)
    pick = (
        lax.broadcasted_iota(jnp.int32, (chunks, windows), 1) // span
        == lax.broadcasted_iota(jnp.int32, (chunks, windows), 0)
    )
    flags[...] = lax.dot_general(
        jnp.where(pick, 1.0, 0.0).astype(jnp.bfloat16),
        spread,
        (((1,), (1,)), ((), ())),
        preferred_element_type=jnp.float32,
    )

    taps = table[...].astype(jnp.bfloat16)
    turn = [lax.rem(w + span - shard, span) for w in range(span)]
    for group in range(groups):
        if group % 3 == 0:
            for copy in large[group : group + 3]:
                copy.wait()
        samples = [traces[4 * group + c, turn[w]] for c in range(4) for w in range(span)]
        spectrum = lax.dot_general(
            taps,
            jnp.concatenate(samples, axis=0),
            (((1,), (1,)), ((), ())),
            preferred_element_type=jnp.float32,
        )
        energy = jnp.sum(spectrum * spectrum, axis=0, keepdims=True) * (1.0 / (2 * nbins))
        gain = lax.rsqrt(energy + 1e-06)
        for part in range(4):
            lanes = slice(part * LANES, (part + 1) * LANES)
            scaled = spectrum[:, lanes] * (
                gain[:, lanes] * flags[pl.ds(4 * group + part, 1), :]
            )
            pieces[group, pl.ds(part, nbins, stride=8), :] = scaled[:nbins]
            pieces[group, pl.ds(4 + part, nbins, stride=8), :] = scaled[nbins:]
        done = pieces[group].astype(white_ref.dtype)
        white_ref[:, group] = done.reshape(nbins // 2, 16, LANES)


def spreading(shape):
    row = lax.broadcasted_iota(jnp.int32, shape, 0).astype(jnp.float32)
    lane = lax.broadcasted_iota(jnp.int32, shape, 1).astype(jnp.float32)
    turn = row * 0.618034 + lane * 0.7548777
    return turn - jnp.floor(turn)


def in_first_group():
    day, half = lax.axis_index("day"), lax.axis_size("day") // 2
    return jnp.where((day % half) ^ (day // half) == 0, 1, 0)


def cross_kernel(channels, factor, pieces_ref, blocks_ref):
    shards = LANES // channels
    rows = pieces_ref.shape[0] // (shards * 2)
    half = LANES // 2
    turned_round = in_first_group()
    pieces = pieces_ref[...].astype(jnp.float32).reshape(shards, rows // 8, 2, 8, LANES)
    lane = lax.broadcasted_iota(jnp.int32, (rows, LANES), 1) // channels
    low = lax.broadcasted_iota(jnp.int32, (channels, LANES), 1) < half
    scale = jnp.exp2(spreading((2 * channels, LANES))) * factor

    for h in range(2):
        parts = [pieces[shards - 1 - s, :, h].reshape(rows, LANES) for s in range(shards)]
        merged = []
        for w in range(shards):
            row_of = parts[-w % shards]
            for g in range(1, shards):
                row_of = jnp.where(lane == g, parts[(g - w) % shards], row_of)
            merged.append(pltpu.roll(row_of, LANES - w * channels, 1) if w else row_of)
        spectra = jnp.concatenate(merged, axis=0)
        turned = pltpu.roll(spectra.reshape(-1, 8, LANES), 4, 1).reshape(spectra.shape)
        place = lax.broadcasted_iota(jnp.int32, spectra.shape, 0)
        turned = jnp.where(place % 8 < 4, turned, -turned)
        cross = lax.dot_general(
            jnp.concatenate([spectra, turned], axis=1).astype(jnp.bfloat16),
            spectra.astype(jnp.bfloat16),
            (((0,), (0,)), ((), ())),
            preferred_element_type=jnp.float32,
        )
        for q in range(4):
            col, row = q // 2, q % 2
            both = []
            for b in range(2):
                first = (2 * b + row) * channels
                real = cross[first : first + channels]
                imag = cross[LANES + first : LANES + first + channels]
                if col == 0:
                    both.append(jnp.where(low, real, pltpu.roll(imag, half, 1)))
                else:
                    both.append(jnp.where(low, pltpu.roll(real, half, 1), imag))
            block = jnp.concatenate(both, axis=0) * scale
            first = pl.multiple_of((4 * h + (q ^ (3 * turned_round))) * 2 * channels, 2 * channels)
            blocks_ref[pl.ds(first, 2 * channels), :] = block.astype(blocks_ref.dtype)


def place_kernel(blocks_ref, out_hbm, out, sems):
    _, bins, _, channels, half = out.shape
    height = 2 * channels
    turned_round = in_first_group()
    scale = jnp.exp2(-spreading((height, 2 * half)))
    copies = [
        pltpu.make_async_copy(out.at[:, q], out_hbm.at[:, q], sems.at[q]) for q in range(bins)
    ]
    for q in range(bins):
        at = [pl.multiple_of((4 * h + (q ^ (3 * turned_round))) * height, height) for h in range(2)]
        pair = [blocks_ref[pl.ds(first, height), :].astype(jnp.float32) for first in at]
        block = (pair[0] + pair[1]) * scale
        for b in range(2):
            out[0, q, b, :, :] = block[b * channels : (b + 1) * channels, :half]
            out[1, q, b, :, :] = block[b * channels : (b + 1) * channels, half:]
        copies[q].start()
    for copy in copies:
        copy.wait()


def two_bins_each(traces, valid):
    windows, channels, length = traces.shape
    days = lax.axis_size("day")
    half = days // 2
    span = LANES // channels
    chunks = windows // span
    groups = chunks // 4
    members = [
        (q, 2 * chip + core)
        for q in (3, 2, 1, 0)
        for core in (1, 0)
        for chip in range(half // 2)[::-1]
    ]
    in_half = [[4 * (h * half + day) + q for q, day in members] for h in range(2)]

    def halves(day):
        return (1, 0) if day // 2 % 2 == 0 else (0, 1)

    def places(day):
        return (3, 2, 1, 0) if day == 0 else (0, 1, 2, 3)

    over_halves = [
        [4 * (h * half + (day ^ h)) + q for h in halves(day) for q in places(day)]
        for day in range(half)
    ]
    tables = [
        [K0 + 4 * (h * half + (day ^ h ^ late)) + q for q, day in members for h in halves(day)]
        for late in range(2)
    ]

    vmem = pl.BlockSpec(memory_space=pltpu.VMEM)
    hbm = pl.BlockSpec(memory_space=pltpu.HBM)
    params = pltpu.CompilerParams(vmem_limit_bytes=32 * 1024 * 1024)
    white = pl.pallas_call(
        whiten_kernel,
        out_shape=jax.ShapeDtypeStruct((F // 2, groups, 16, LANES), jnp.bfloat16),
        in_specs=[hbm] * 3,
        out_specs=vmem,
        scratch_shapes=[
            pltpu.VMEM((chunks, span, channels, length), jnp.bfloat16),
            pltpu.VMEM((channels, windows), jnp.int32),
            pltpu.VMEM((2 * F, length), jnp.float32),
            pltpu.VMEM((chunks, LANES), jnp.float32),
            pltpu.VMEM((groups, 8 * F, LANES), jnp.float32),
            pltpu.SemaphoreType.DMA((groups + 2,)),
        ],
        compiler_params=params,
        name="whiten",
    )(
        *(
            pltpu.with_memory_space_constraint(operand, pltpu.HBM)
            for operand in (
                traces.reshape(chunks, span, channels, length),
                valid.T,
                np.stack([dft_rows(L, bins).astype(np.float32) for bins in tables]),
            )
        )
    )
    everyone = ("day", "col", "row")
    white = white.reshape(-1, LANES)
    pieces = lax.all_to_all(white, everyone, 0, 0, axis_index_groups=in_half, tiled=True)
    blocks = pl.pallas_call(
        functools.partial(cross_kernel, channels, 1.0 / math.sqrt(windows * days)),
        out_shape=jax.ShapeDtypeStruct((8 * 2 * channels, LANES), jnp.bfloat16),
        in_specs=[vmem],
        out_specs=vmem,
        compiler_params=params,
        name="cross",
    )(pieces)
    placed = lax.all_to_all(blocks, everyone, 0, 0, axis_index_groups=over_halves, tiled=True)
    return pl.pallas_call(
        place_kernel,
        out_shape=jax.ShapeDtypeStruct((2, 4, 2, channels, LANES // 2), jnp.float32),
        in_specs=[vmem],
        out_specs=hbm,
        scratch_shapes=[
            pltpu.VMEM((2, 4, 2, channels, LANES // 2), jnp.float32),
            pltpu.SemaphoreType.DMA((4,)),
        ],
        compiler_params=params,
        name="place",
    )(placed)


def pair_maker(receiver_spectra, source_part):
    nbins, doubled, width = source_part.shape
    halves = source_part.reshape(nbins, 2, doubled // 2, width)
    turned = jnp.concatenate([halves[:, 1], -halves[:, 0]], axis=1)
    real_part = jnp.einsum(
        "fwi,fwj->fij", source_part, receiver_spectra, preferred_element_type=jnp.float32
    )
    imag_part = jnp.einsum(
        "fwi,fwj->fij", turned, receiver_spectra, preferred_element_type=jnp.float32
    )
    return jnp.stack([real_part, imag_part])


def gathered(traces, valid):
    windows_here, channels_here, length = traces.shape
    spectrum = jnp.dot(
        traces.reshape(windows_here * channels_here, length),
        jnp.asarray(dft_rows(L, range(K0, K0 + F)).T),
        preferred_element_type=jnp.float32,
    )
    energy = jnp.mean(spectrum * spectrum, axis=1, keepdims=True)
    scaled = (
        spectrum
        * lax.rsqrt(energy + 1e-06)
        * valid.reshape(windows_here * channels_here, 1).astype(jnp.float32)
    )
    white = jnp.transpose(
        scaled.astype(jnp.bfloat16).reshape(windows_here, channels_here, 2, F), (3, 2, 0, 1)
    )
    day_count = lax.axis_size("day")
    own_spectra = white.reshape(F, 2 * windows_here, channels_here)
    receiver_spectra = lax.all_gather(own_spectra, "row", axis=2, tiled=True)
    partial_terms = pair_maker(
        receiver_spectra, lax.all_gather(own_spectra, "col", axis=2, tiled=True)
    )
    summed = lax.psum_scatter(partial_terms, "day", scatter_dimension=1, tiled=True)
    stacked = summed * (1.0 / math.sqrt(windows_here * day_count))
    col_count = lax.axis_size("col")
    return stacked.reshape(2, stacked.shape[1], col_count, channels_here, stacked.shape[3])


def shards(traces, valid):
    windows, channels, _ = traces.shape
    cols, rows = lax.axis_size("col"), lax.axis_size("row")
    owners = lax.axis_size("day") * cols * rows
    fits = (
        owners == F
        and cols == 2
        and rows == 2
        and cols * rows * channels == LANES
        and windows * channels % (4 * LANES) == 0
    )
    return two_bins_each(traces, valid) if fits else gathered(traces, valid)


def solution(mesh):
    placed = (P("day", ("col", "row"), None), P("day", ("col", "row")))
    return jax.shard_map(
        shards,
        mesh=mesh,
        in_specs=placed,
        out_specs=P(None, "day", None, "row", "col"),
        check_vma=False,
    )
```

```python
import functools
import math

import jax
import jax.numpy as jnp
import numpy as np
from jax import lax
from jax.experimental import pallas as pl
from jax.experimental.pallas import tpu as pltpu
from jax.sharding import PartitionSpec as P

L = 256
F = 32
K0 = 16
LANES = 128


def dft_rows(length, bins):
    sample = np.arange(length, dtype=np.int32)
    bins = np.asarray(bins, dtype=np.int32)
    angle = (sample[None, :] * bins[:, None] % length).astype(np.float32) * np.float32(
        2.0 * math.pi / length
    )
    taper = np.float32(0.5) - np.float32(0.5) * np.cos(
        (sample.astype(np.float32) + np.float32(0.5)) * np.float32(2.0 * math.pi / length)
    )
    table = np.concatenate([taper * np.cos(angle), -taper * np.sin(angle)], axis=0)
    return table.astype(jnp.bfloat16)


def whiten_kernel(
    traces_hbm, valid_hbm, table_hbm, white_ref, traces, valid, table, flags, pieces, sems
):
    chunks, span, channels, length = traces.shape
    nbins = table.shape[0] // 2
    windows = chunks * span
    groups = chunks // 4
    shard = 2 * lax.axis_index("col") + lax.axis_index("row")
    late = lax.axis_index("day") // (lax.axis_size("day") // 2)

    small = [
        pltpu.make_async_copy(valid_hbm, valid, sems.at[groups]),
        pltpu.make_async_copy(table_hbm.at[late], table, sems.at[groups + 1]),
    ]
    large = [
        pltpu.make_async_copy(
            traces_hbm.at[pl.ds(4 * g, 4)], traces.at[pl.ds(4 * g, 4)], sems.at[g]
        )
        for g in range(groups)
    ]
    for copy in small + large:
        copy.start()
    for copy in small:
        copy.wait()

    spread = jnp.concatenate([valid[...].astype(jnp.float32)] * span, axis=0)
    place = lax.broadcasted_iota(jnp.int32, spread.shape, 0) // channels
    window = lax.broadcasted_iota(jnp.int32, spread.shape, 1)
    spread = jnp.where((window + shard) % span == place, spread, 0.0).astype(jnp.bfloat16)
    pick = (
        lax.broadcasted_iota(jnp.int32, (chunks, windows), 1) // span
        == lax.broadcasted_iota(jnp.int32, (chunks, windows), 0)
    )
    flags[...] = lax.dot_general(
        jnp.where(pick, 1.0, 0.0).astype(jnp.bfloat16),
        spread,
        (((1,), (1,)), ((), ())),
        preferred_element_type=jnp.float32,
    )

    taps = table[...].astype(jnp.bfloat16)
    turn = [lax.rem(w + span - shard, span) for w in range(span)]
    for group in range(groups):
        if group % 3 == 0:
            for copy in large[group : group + 3]:
                copy.wait()
        samples = [traces[4 * group + c, turn[w]] for c in range(4) for w in range(span)]
        spectrum = lax.dot_general(
            taps,
            jnp.concatenate(samples, axis=0),
            (((1,), (1,)), ((), ())),
            preferred_element_type=jnp.float32,
        )
        energy = jnp.sum(spectrum * spectrum, axis=0, keepdims=True) * (1.0 / (2 * nbins))
        gain = lax.rsqrt(energy + 1e-06)
        for part in range(4):
            lanes = slice(part * LANES, (part + 1) * LANES)
            scaled = spectrum[:, lanes] * (
                gain[:, lanes] * flags[pl.ds(4 * group + part, 1), :]
            )
            pieces[group, pl.ds(part, nbins, stride=8), :] = scaled[:nbins]
            pieces[group, pl.ds(4 + part, nbins, stride=8), :] = scaled[nbins:]
        done = pieces[group].astype(white_ref.dtype)
        white_ref[:, group] = done.reshape(nbins // 2, 16, LANES)


def spreading(shape):
    row = lax.broadcasted_iota(jnp.int32, shape, 0).astype(jnp.float32)
    lane = lax.broadcasted_iota(jnp.int32, shape, 1).astype(jnp.float32)
    turn = row * 0.618034 + lane * 0.7548777
    return turn - jnp.floor(turn)


def cross_kernel(channels, factor, pieces_ref, blocks_ref):
    shards = LANES // channels
    rows = pieces_ref.shape[0] // (shards * 2)
    half = LANES // 2
    pieces = pieces_ref[...].astype(jnp.float32).reshape(shards, rows // 8, 2, 8, LANES)
    lane = lax.broadcasted_iota(jnp.int32, (rows, LANES), 1) // channels
    low = lax.broadcasted_iota(jnp.int32, (channels, LANES), 1) < half
    scale = jnp.exp2(spreading((2 * channels, LANES))) * factor

    for h in range(2):
        parts = [pieces[shards - 1 - s, :, h].reshape(rows, LANES) for s in range(shards)]
        merged = []
        for w in range(shards):
            row_of = parts[-w % shards]
            for g in range(1, shards):
                row_of = jnp.where(lane == g, parts[(g - w) % shards], row_of)
            merged.append(pltpu.roll(row_of, LANES - w * channels, 1) if w else row_of)
        spectra = jnp.concatenate(merged, axis=0)
        turned = pltpu.roll(spectra.reshape(-1, 8, LANES), 4, 1).reshape(spectra.shape)
        place = lax.broadcasted_iota(jnp.int32, spectra.shape, 0)
        turned = jnp.where(place % 8 < 4, turned, -turned)
        cross = lax.dot_general(
            jnp.concatenate([spectra, turned], axis=1).astype(jnp.bfloat16),
            spectra.astype(jnp.bfloat16),
            (((0,), (0,)), ((), ())),
            preferred_element_type=jnp.float32,
        )
        for q in range(4):
            col, row = q // 2, q % 2
            both = []
            for b in range(2):
                first = (2 * b + row) * channels
                real = cross[first : first + channels]
                imag = cross[LANES + first : LANES + first + channels]
                if col == 0:
                    both.append(jnp.where(low, real, pltpu.roll(imag, half, 1)))
                else:
                    both.append(jnp.where(low, pltpu.roll(real, half, 1), imag))
            block = jnp.concatenate(both, axis=0) * scale
            first = (4 * h + 3 - q) * 2 * channels
            blocks_ref[pl.ds(first, 2 * channels), :] = block.astype(blocks_ref.dtype)


def place_kernel(blocks_ref, out_hbm, out, sems):
    _, bins, _, channels, half = out.shape
    height = 2 * channels
    scale = jnp.exp2(-spreading((height, 2 * half)))
    copies = [
        pltpu.make_async_copy(out.at[:, q], out_hbm.at[:, q], sems.at[q]) for q in range(bins)
    ]
    for q in range(bins):
        pair = [
            blocks_ref[pl.ds((4 * h + 3 - q) * height, height), :].astype(jnp.float32)
            for h in range(2)
        ]
        block = (pair[0] + pair[1]) * scale
        for b in range(2):
            out[0, q, b, :, :] = block[b * channels : (b + 1) * channels, :half]
            out[1, q, b, :, :] = block[b * channels : (b + 1) * channels, half:]
        copies[q].start()
    for copy in copies:
        copy.wait()


def two_bins_each(traces, valid):
    windows, channels, length = traces.shape
    days = lax.axis_size("day")
    half = days // 2
    span = LANES // channels
    chunks = windows // span
    groups = chunks // 4
    chips = [day for core in range(2) for day in range(core, half, 2)]
    members = [(q, day) for q in (3, 2, 1, 0) for day in range(half)[::-1]]
    in_half = [[4 * (h * half + day) + q for q, day in members] for h in range(2)]

    def halves(day):
        return (1, 0) if day // 2 % 2 == 0 else (0, 1)

    over_halves = [
        [4 * (h * half + (day ^ h)) + q for h in halves(day) for q in (3, 2, 1, 0)] for day in chips
    ]
    tables = [
        [K0 + 4 * (h * half + (day ^ h ^ late)) + q for q, day in members for h in halves(day)]
        for late in range(2)
    ]

    vmem = pl.BlockSpec(memory_space=pltpu.VMEM)
    hbm = pl.BlockSpec(memory_space=pltpu.HBM)
    params = pltpu.CompilerParams(vmem_limit_bytes=32 * 1024 * 1024)
    white = pl.pallas_call(
        whiten_kernel,
        out_shape=jax.ShapeDtypeStruct((F // 2, groups, 16, LANES), jnp.bfloat16),
        in_specs=[hbm] * 3,
        out_specs=vmem,
        scratch_shapes=[
            pltpu.VMEM((chunks, span, channels, length), jnp.bfloat16),
            pltpu.VMEM((channels, windows), jnp.int32),
            pltpu.VMEM((2 * F, length), jnp.float32),
            pltpu.VMEM((chunks, LANES), jnp.float32),
            pltpu.VMEM((groups, 8 * F, LANES), jnp.float32),
            pltpu.SemaphoreType.DMA((groups + 2,)),
        ],
        compiler_params=params,
        name="whiten",
    )(
        *(
            pltpu.with_memory_space_constraint(operand, pltpu.HBM)
            for operand in (
                traces.reshape(chunks, span, channels, length),
                valid.T,
                np.stack([dft_rows(L, bins).astype(np.float32) for bins in tables]),
            )
        )
    )
    everyone = ("day", "col", "row")
    white = white.reshape(-1, LANES)
    pieces = lax.all_to_all(white, everyone, 0, 0, axis_index_groups=in_half, tiled=True)
    blocks = pl.pallas_call(
        functools.partial(cross_kernel, channels, 1.0 / math.sqrt(windows * days)),
        out_shape=jax.ShapeDtypeStruct((8 * 2 * channels, LANES), jnp.bfloat16),
        in_specs=[vmem],
        out_specs=vmem,
        compiler_params=params,
        name="cross",
    )(pieces)
    placed = lax.all_to_all(blocks, everyone, 0, 0, axis_index_groups=over_halves, tiled=True)
    return pl.pallas_call(
        place_kernel,
        out_shape=jax.ShapeDtypeStruct((2, 4, 2, channels, LANES // 2), jnp.float32),
        in_specs=[vmem],
        out_specs=hbm,
        scratch_shapes=[
            pltpu.VMEM((2, 4, 2, channels, LANES // 2), jnp.float32),
            pltpu.SemaphoreType.DMA((4,)),
        ],
        compiler_params=params,
        name="place",
    )(placed)


def pair_maker(receiver_spectra, source_part):
    nbins, doubled, width = source_part.shape
    halves = source_part.reshape(nbins, 2, doubled // 2, width)
    turned = jnp.concatenate([halves[:, 1], -halves[:, 0]], axis=1)
    real_part = jnp.einsum(
        "fwi,fwj->fij", source_part, receiver_spectra, preferred_element_type=jnp.float32
    )
    imag_part = jnp.einsum(
        "fwi,fwj->fij", turned, receiver_spectra, preferred_element_type=jnp.float32
    )
    return jnp.stack([real_part, imag_part])


def gathered(traces, valid):
    windows_here, channels_here, length = traces.shape
    spectrum = jnp.dot(
        traces.reshape(windows_here * channels_here, length),
        jnp.asarray(dft_rows(L, range(K0, K0 + F)).T),
        preferred_element_type=jnp.float32,
    )
    energy = jnp.mean(spectrum * spectrum, axis=1, keepdims=True)
    scaled = (
        spectrum
        * lax.rsqrt(energy + 1e-06)
        * valid.reshape(windows_here * channels_here, 1).astype(jnp.float32)
    )
    white = jnp.transpose(
        scaled.astype(jnp.bfloat16).reshape(windows_here, channels_here, 2, F), (3, 2, 0, 1)
    )
    day_count = lax.axis_size("day")
    own_spectra = white.reshape(F, 2 * windows_here, channels_here)
    receiver_spectra = lax.all_gather(own_spectra, "row", axis=2, tiled=True)
    partial_terms = pair_maker(
        receiver_spectra, lax.all_gather(own_spectra, "col", axis=2, tiled=True)
    )
    summed = lax.psum_scatter(partial_terms, "day", scatter_dimension=1, tiled=True)
    stacked = summed * (1.0 / math.sqrt(windows_here * day_count))
    col_count = lax.axis_size("col")
    return stacked.reshape(2, stacked.shape[1], col_count, channels_here, stacked.shape[3])


def shards(traces, valid):
    windows, channels, _ = traces.shape
    cols, rows = lax.axis_size("col"), lax.axis_size("row")
    owners = lax.axis_size("day") * cols * rows
    fits = (
        owners == F
        and cols == 2
        and rows == 2
        and cols * rows * channels == LANES
        and windows * channels % (4 * LANES) == 0
    )
    return two_bins_each(traces, valid) if fits else gathered(traces, valid)


def solution(mesh):
    placed = (P("day", ("col", "row"), None), P("day", ("col", "row")))
    return jax.shard_map(
        shards,
        mesh=mesh,
        in_specs=placed,
        out_specs=P(None, "day", None, "row", "col"),
        check_vma=False,
    )
```

```python
import functools
import math

import jax
import jax.numpy as jnp
import numpy as np
from jax import lax
from jax.experimental import pallas as pl
from jax.experimental.pallas import tpu as pltpu
from jax.sharding import PartitionSpec as P

L = 256
F = 32
K0 = 16
LANES = 128


def dft_rows(length, bins):
    sample = np.arange(length, dtype=np.int32)
    bins = np.asarray(bins, dtype=np.int32)
    angle = (sample[None, :] * bins[:, None] % length).astype(np.float32) * np.float32(
        2.0 * math.pi / length
    )
    taper = np.float32(0.5) - np.float32(0.5) * np.cos(
        (sample.astype(np.float32) + np.float32(0.5)) * np.float32(2.0 * math.pi / length)
    )
    table = np.concatenate([taper * np.cos(angle), -taper * np.sin(angle)], axis=0)
    return table.astype(jnp.bfloat16)


def whiten_kernel(
    traces_hbm, valid_hbm, table_hbm, white_ref, traces, valid, table, flags, pieces, sems
):
    chunks, span, channels, length = traces.shape
    nbins = table.shape[0] // 2
    windows = chunks * span
    groups = chunks // 4
    shard = 2 * lax.axis_index("col") + lax.axis_index("row")
    late = lax.axis_index("day") // (lax.axis_size("day") // 2)

    small = [
        pltpu.make_async_copy(valid_hbm, valid, sems.at[groups]),
        pltpu.make_async_copy(table_hbm.at[late], table, sems.at[groups + 1]),
    ]
    large = [
        pltpu.make_async_copy(
            traces_hbm.at[pl.ds(4 * g, 4)], traces.at[pl.ds(4 * g, 4)], sems.at[g]
        )
        for g in range(groups)
    ]
    for copy in small + large:
        copy.start()
    for copy in small + large[:3]:
        copy.wait()

    spread = jnp.concatenate([valid[...].astype(jnp.float32)] * span, axis=0)
    place = lax.broadcasted_iota(jnp.int32, spread.shape, 0) // channels
    window = lax.broadcasted_iota(jnp.int32, spread.shape, 1)
    spread = jnp.where((window + shard) % span == place, spread, 0.0).astype(jnp.bfloat16)
    pick = (
        lax.broadcasted_iota(jnp.int32, (chunks, windows), 1) // span
        == lax.broadcasted_iota(jnp.int32, (chunks, windows), 0)
    )
    flags[...] = lax.dot_general(
        jnp.where(pick, 1.0, 0.0).astype(jnp.bfloat16),
        spread,
        (((1,), (1,)), ((), ())),
        preferred_element_type=jnp.float32,
    )

    taps = table[...].astype(jnp.bfloat16)
    turn = [lax.rem(w + span - shard, span) for w in range(span)]
    for group in range(groups):
        if group and group % 3 == 0:
            for copy in large[group : group + 3]:
                copy.wait()
        samples = [traces[4 * group + c, turn[w]] for c in range(4) for w in range(span)]
        spectrum = lax.dot_general(
            taps,
            jnp.concatenate(samples, axis=0),
            (((1,), (1,)), ((), ())),
            preferred_element_type=jnp.float32,
        )
        energy = jnp.sum(spectrum * spectrum, axis=0, keepdims=True) * (1.0 / (2 * nbins))
        gain = lax.rsqrt(energy + 1e-06)
        for part in range(4):
            lanes = slice(part * LANES, (part + 1) * LANES)
            scaled = spectrum[:, lanes] * (
                gain[:, lanes] * flags[pl.ds(4 * group + part, 1), :]
            )
            pieces[group, pl.ds(part, nbins, stride=8), :] = scaled[:nbins]
            pieces[group, pl.ds(4 + part, nbins, stride=8), :] = scaled[nbins:]
        done = pieces[group, pl.ds(0, 8 * nbins), :].astype(white_ref.dtype)
        white_ref[:, group] = done.reshape(nbins // 2, 16, LANES)


def spreading(shape):
    row = lax.broadcasted_iota(jnp.int32, shape, 0).astype(jnp.float32)
    lane = lax.broadcasted_iota(jnp.int32, shape, 1).astype(jnp.float32)
    turn = row * 0.618034 + lane * 0.7548777
    return turn - jnp.floor(turn)


def cross_kernel(channels, factor, pieces_ref, blocks_ref):
    shards = LANES // channels
    rows = pieces_ref.shape[0] // (shards * 2)
    half = LANES // 2
    pieces = pieces_ref[...].astype(jnp.float32).reshape(shards, rows // 8, 2, 8, LANES)
    lane = lax.broadcasted_iota(jnp.int32, (rows, LANES), 1) // channels
    low = lax.broadcasted_iota(jnp.int32, (channels, LANES), 1) < half
    scale = jnp.exp2(spreading((2 * channels, LANES))) * factor

    for h in range(2):
        parts = [pieces[shards - 1 - s, :, h].reshape(rows, LANES) for s in range(shards)]
        merged = []
        for w in range(shards):
            row_of = parts[-w % shards]
            for g in range(1, shards):
                row_of = jnp.where(lane == g, parts[(g - w) % shards], row_of)
            merged.append(pltpu.roll(row_of, LANES - w * channels, 1) if w else row_of)
        spectra = jnp.concatenate(merged, axis=0)
        turned = pltpu.roll(spectra.reshape(-1, 8, LANES), 4, 1).reshape(spectra.shape)
        place = lax.broadcasted_iota(jnp.int32, spectra.shape, 0)
        turned = jnp.where(place % 8 < 4, turned, -turned)
        cross = lax.dot_general(
            jnp.concatenate([spectra, turned], axis=1).astype(jnp.bfloat16),
            spectra.astype(jnp.bfloat16),
            (((0,), (0,)), ((), ())),
            preferred_element_type=jnp.float32,
        )
        for q in range(4):
            col, row = q // 2, q % 2
            both = []
            for b in range(2):
                first = (2 * b + row) * channels
                real = cross[first : first + channels]
                imag = cross[LANES + first : LANES + first + channels]
                if col == 0:
                    both.append(jnp.where(low, real, pltpu.roll(imag, half, 1)))
                else:
                    both.append(jnp.where(low, pltpu.roll(real, half, 1), imag))
            block = jnp.concatenate(both, axis=0) * scale
            first = (4 * h + 3 - q) * 2 * channels
            blocks_ref[pl.ds(first, 2 * channels), :] = block.astype(blocks_ref.dtype)


def place_kernel(blocks_ref, out_hbm, out, sems):
    _, bins, _, channels, half = out.shape
    height = 2 * channels
    scale = jnp.exp2(-spreading((height, 2 * half)))
    copies = [
        pltpu.make_async_copy(out.at[:, q], out_hbm.at[:, q], sems.at[q]) for q in range(bins)
    ]
    for q in range(bins):
        pair = [
            blocks_ref[pl.ds((4 * h + 3 - q) * height, height), :].astype(jnp.float32)
            for h in range(2)
        ]
        block = (pair[0] + pair[1]) * scale
        for b in range(2):
            out[0, q, b, :, :] = block[b * channels : (b + 1) * channels, :half]
            out[1, q, b, :, :] = block[b * channels : (b + 1) * channels, half:]
        copies[q].start()
    for copy in copies:
        copy.wait()


def two_bins_each(traces, valid):
    windows, channels, length = traces.shape
    days = lax.axis_size("day")
    half = days // 2
    span = LANES // channels
    chunks = windows // span
    groups = chunks // 4
    chips = [day for core in range(2) for day in range(core, half, 2)]
    members = [(q, day) for q in (3, 2, 1, 0) for day in range(half)[::-1]]
    in_half = [[4 * (h * half + day) + q for q, day in members] for h in range(2)]

    def halves(day):
        return (1, 0) if day // 2 % 2 == 0 else (0, 1)

    over_halves = [
        [4 * (h * half + (day ^ h)) + q for h in halves(day) for q in (3, 2, 1, 0)] for day in chips
    ]
    tables = [
        [K0 + 4 * (h * half + (day ^ h ^ late)) + q for q, day in members for h in halves(day)]
        for late in range(2)
    ]

    vmem = pl.BlockSpec(memory_space=pltpu.VMEM)
    hbm = pl.BlockSpec(memory_space=pltpu.HBM)
    params = pltpu.CompilerParams(vmem_limit_bytes=32 * 1024 * 1024)
    white = pl.pallas_call(
        whiten_kernel,
        out_shape=jax.ShapeDtypeStruct((F // 2, groups, 16, LANES), jnp.bfloat16),
        in_specs=[hbm] * 3,
        out_specs=vmem,
        scratch_shapes=[
            pltpu.VMEM((chunks, span, channels, length), jnp.bfloat16),
            pltpu.VMEM((channels, windows), jnp.int32),
            pltpu.VMEM((2 * F, length), jnp.float32),
            pltpu.VMEM((chunks, LANES), jnp.float32),
            pltpu.VMEM((groups, 8 * F + 8, LANES), jnp.float32),
            pltpu.SemaphoreType.DMA((groups + 2,)),
        ],
        compiler_params=params,
        name="whiten",
    )(
        *(
            pltpu.with_memory_space_constraint(operand, pltpu.HBM)
            for operand in (
                traces.reshape(chunks, span, channels, length),
                valid.T,
                np.stack([dft_rows(L, bins).astype(np.float32) for bins in tables]),
            )
        )
    )
    everyone = ("day", "col", "row")
    white = white.reshape(-1, LANES)
    pieces = lax.all_to_all(white, everyone, 0, 0, axis_index_groups=in_half, tiled=True)
    blocks = pl.pallas_call(
        functools.partial(cross_kernel, channels, 1.0 / math.sqrt(windows * days)),
        out_shape=jax.ShapeDtypeStruct((8 * 2 * channels, LANES), jnp.bfloat16),
        in_specs=[vmem],
        out_specs=vmem,
        compiler_params=params,
        name="cross",
    )(pieces)
    placed = lax.all_to_all(blocks, everyone, 0, 0, axis_index_groups=over_halves, tiled=True)
    return pl.pallas_call(
        place_kernel,
        out_shape=jax.ShapeDtypeStruct((2, 4, 2, channels, LANES // 2), jnp.float32),
        in_specs=[vmem],
        out_specs=hbm,
        scratch_shapes=[
            pltpu.VMEM((2, 4, 2, channels, LANES // 2), jnp.float32),
            pltpu.SemaphoreType.DMA((4,)),
        ],
        compiler_params=params,
        name="place",
    )(placed)


def pair_maker(receiver_spectra, source_part):
    nbins, doubled, width = source_part.shape
    halves = source_part.reshape(nbins, 2, doubled // 2, width)
    turned = jnp.concatenate([halves[:, 1], -halves[:, 0]], axis=1)
    real_part = jnp.einsum(
        "fwi,fwj->fij", source_part, receiver_spectra, preferred_element_type=jnp.float32
    )
    imag_part = jnp.einsum(
        "fwi,fwj->fij", turned, receiver_spectra, preferred_element_type=jnp.float32
    )
    return jnp.stack([real_part, imag_part])


def gathered(traces, valid):
    windows_here, channels_here, length = traces.shape
    spectrum = jnp.dot(
        traces.reshape(windows_here * channels_here, length),
        jnp.asarray(dft_rows(L, range(K0, K0 + F)).T),
        preferred_element_type=jnp.float32,
    )
    energy = jnp.mean(spectrum * spectrum, axis=1, keepdims=True)
    scaled = (
        spectrum
        * lax.rsqrt(energy + 1e-06)
        * valid.reshape(windows_here * channels_here, 1).astype(jnp.float32)
    )
    white = jnp.transpose(
        scaled.astype(jnp.bfloat16).reshape(windows_here, channels_here, 2, F), (3, 2, 0, 1)
    )
    day_count = lax.axis_size("day")
    own_spectra = white.reshape(F, 2 * windows_here, channels_here)
    receiver_spectra = lax.all_gather(own_spectra, "row", axis=2, tiled=True)
    partial_terms = pair_maker(
        receiver_spectra, lax.all_gather(own_spectra, "col", axis=2, tiled=True)
    )
    summed = lax.psum_scatter(partial_terms, "day", scatter_dimension=1, tiled=True)
    stacked = summed * (1.0 / math.sqrt(windows_here * day_count))
    col_count = lax.axis_size("col")
    return stacked.reshape(2, stacked.shape[1], col_count, channels_here, stacked.shape[3])


def shards(traces, valid):
    windows, channels, _ = traces.shape
    cols, rows = lax.axis_size("col"), lax.axis_size("row")
    owners = lax.axis_size("day") * cols * rows
    fits = (
        owners == F
        and cols == 2
        and rows == 2
        and cols * rows * channels == LANES
        and windows * channels % (4 * LANES) == 0
    )
    return two_bins_each(traces, valid) if fits else gathered(traces, valid)


def solution(mesh):
    placed = (P("day", ("col", "row"), None), P("day", ("col", "row")))
    return jax.shard_map(
        shards,
        mesh=mesh,
        in_specs=placed,
        out_specs=P(None, "day", None, "row", "col"),
        check_vma=False,
    )
```
